512 devices in a mesh: row: 64 (over x, z_lo, y), col: 8 (over z_hi, core).
Axes of the slice: x: 4, y: 4, z: 16 (z_hi: 4, z_lo: 4; z = z_hi * 4 + z_lo), core: 2. Of those that a mesh axis runs over, the one named last changes fastest.
Arguments:
- tokens: bfloat16 [320, 8192], P('row', 'col'), may hold values from -6 to 6
- cotangent: bfloat16 [320, 8192], P('row', 'col'), may hold values from -6 to 6
- gate_weight: bfloat16 [8192, 28672], P('col', 'row'), may hold values from -0.0625 to 0.0625
- up_weight: bfloat16 [8192, 28672], P('col', 'row'), may hold values from -0.0625 to 0.0625
- down_weight: bfloat16 [28672, 8192], P('row', 'col'), may hold values from -0.03125 to 0.03125
- old_in_hidden: bfloat16 [2, 8192, 128], P(None, 'col'), may hold values from -0.0625 to 0.0625
- old_out_hidden: bfloat16 [2, 128, 28672], P(None, None, 'row'), may hold values from -0.5 to 0.5
- old_in_down: bfloat16 [28672, 128], P('row'), may hold values from -0.03125 to 0.03125
- old_out_down: bfloat16 [128, 8192], P(None, 'col'), may hold values from -0.5 to 0.5
- new_in_hidden: bfloat16 [2, 8192, 128], P(None, 'col'), may hold values from -0.0625 to 0.0625
- new_in_down: bfloat16 [28672, 128], P('row'), may hold values from -0.03125 to 0.03125
- first_hidden: float32 [2, 128, 28672], P(None, 'col', 'row'), may hold values from -4 to 4
- second_hidden: float32 [2, 128, 28672], P(None, 'col', 'row'), may hold values from 0.01 to 1
- first_down: float32 [128, 8192], P('row', 'col'), may hold values from -4 to 4
- second_down: float32 [128, 8192], P('row', 'col'), may hold values from 0.01 to 1
- keep_hidden: int32 [2, 28672], P(None, 'row'), may hold values 0 or 1
- keep_down: int32 [8192], P('col'), may hold values 0 or 1
Outputs:
- input_grad: bfloat16 [320, 8192], P('row', 'col')
- new_first_hidden: float32 [2, 128, 28672], P(None, 'col', 'row')
- new_second_hidden: float32 [2, 128, 28672], P(None, 'col', 'row')
- new_first_down: float32 [128, 8192], P('row', 'col')
- new_second_down: float32 [128, 8192], P('row', 'col')
The draws below stay inside these ranges and needn't reach their ends.
All inputs are finite; a program needn't handle non-finite values. No bound on the sum of `keep_hidden` or of `keep_down` on one device may be relied on, other than what follows from the above.
Results may differ from the reference program's by a relative error of at most 0.0072.
Values may be sent and summed in bfloat16 or wider, within the bound.
A program may use at most 64 MiB of HBM per device.

```python
import math
import jax
import jax.numpy as jnp
from jax import lax

D = 8192
FF = 28672
R = 128
TOKENS = 320


def with_ends(drawn, stream_key, smallest, high):
    dims = drawn.shape
    spot = [jax.random.randint(jax.random.fold_in(stream_key, axis), (), 0, dims[axis]) for axis in range(len(dims))]
    drawn = drawn.at[tuple(spot)].set(smallest)
    longest = dims.index(max(dims))
    spot[longest] = (spot[longest] + 1) % dims[longest]
    return drawn.at[tuple(spot)].set(high)


def shard_levels(own_key, dims, split, least, top_value):
    def one(dim, shards_of):
        heights = jax.random.uniform(jax.random.fold_in(jax.random.fold_in(own_key, 6), dim), (shards_of,), jnp.float32, least / len(split), top_value / len(split))
        return jnp.repeat(jnp.exp(heights), dims[dim] // shards_of).reshape((-1,) + (1,) * (len(dims) - dim - 1))

    loudness = one(*split[0])
    for cut in split[1:]:
        loudness = loudness * one(*cut)
    return loudness


def scatter_about(stream_key, shape, deviation, bound, split=(), dtype=jnp.bfloat16):
    result = jax.random.normal(stream_key, shape, jnp.float32) * deviation
    if len(split) > 0:
        result = shard_levels(stream_key, shape, split, -0.22, 0.18) * result
    return jnp.clip(result, min=-bound, max=bound).astype(dtype)


def setup_inputs(seed: int = 0) -> dict:
    key_of = jax.random.split(jax.random.key(seed), 18)
    return {
        "tokens": scatter_about(key_of[0], (TOKENS, D), 1.0, 6.0, ((0, 64), (1, 8))),
        "cotangent": scatter_about(key_of[1], (TOKENS, D), 1.0, 6.0, ((0, 64), (1, 8))),
        "gate_weight": scatter_about(key_of[2], (D, FF), D ** -0.5, 0.0625, ((0, 8), (1, 64))),
        "up_weight": scatter_about(key_of[3], (D, FF), D ** -0.5, 0.0625, ((0, 8), (1, 64))),
        "down_weight": scatter_about(key_of[4], (FF, D), FF ** -0.5, 0.03125, ((0, 64), (1, 8))),
        "old_in_hidden": scatter_about(key_of[5], (2, D, R), D ** -0.5, 0.0625, ((1, 8),)),
        "old_out_hidden": scatter_about(key_of[6], (2, R, FF), R ** -0.5, 0.5, ((2, 64),)),
        "old_in_down": scatter_about(key_of[7], (FF, R), FF ** -0.5, 0.03125, ((0, 64),)),
        "old_out_down": scatter_about(key_of[8], (R, D), R ** -0.5, 0.5, ((1, 8),)),
        "new_in_hidden": scatter_about(key_of[9], (2, D, R), D ** -0.5, 0.0625, ((1, 8),)),
        "new_in_down": scatter_about(key_of[10], (FF, R), FF ** -0.5, 0.03125, ((0, 64),)),
        "first_hidden": scatter_about(key_of[11], (2, R, FF), 0.5, 4.0, ((1, 8), (2, 64)), jnp.float32),
        "second_hidden": jnp.clip(jnp.exp(math.log(1.0) - 4.6051702 * jax.random.uniform(key_of[12], (2, R, FF), jnp.float32) ** shard_levels(key_of[12], (2, R, FF), ((1, 8), (2, 64)), -0.2, 0.2)), 0.01, 1.0),
        "first_down": scatter_about(key_of[13], (R, D), 0.5, 4.0, ((0, 64), (1, 8)), jnp.float32),
        "second_down": jnp.clip(jnp.exp(math.log(1.0) - 4.6051702 * jax.random.uniform(key_of[14], (R, D), jnp.float32) ** shard_levels(key_of[14], (R, D), ((0, 64), (1, 8)), -0.2, 0.2)), 0.01, 1.0),
        "keep_hidden": with_ends((jax.random.randint(key_of[15], (2, FF), 0, 2) < 1).astype(jnp.int32), jax.random.fold_in(key_of[15], 1), 0, 1),
        "keep_down": with_ends((jax.random.randint(key_of[16], (D,), 0, 2) < 1).astype(jnp.int32), jax.random.fold_in(key_of[16], 1), 0, 1),
    }


adapter_scale = 0.25


def merge_weight(frozen_weight, left, right):
    weight_increment = jnp.dot(left, right, preferred_element_type=jnp.float32)
    return (frozen_weight.astype(jnp.float32) + adapter_scale * weight_increment).astype(jnp.bfloat16)


def reference(tokens, cotangent, gate_weight, up_weight, down_weight, old_in_hidden, old_out_hidden, old_in_down, old_out_down, new_in_hidden, new_in_down, first_hidden, second_hidden, first_down, second_down, keep_hidden, keep_down):
    merged_gate = merge_weight(gate_weight, old_in_hidden[0], old_out_hidden[0])
    merged_up = merge_weight(up_weight, old_in_hidden[1], old_out_hidden[1])
    merged_down = merge_weight(down_weight, old_in_down, old_out_down)
    gate = jnp.dot(tokens, merged_gate, preferred_element_type=jnp.float32)
    up = jnp.dot(tokens, merged_up, preferred_element_type=jnp.float32)
    gate_rank_factor = jnp.dot(tokens, new_in_hidden[0], preferred_element_type=jnp.float32).astype(jnp.bfloat16)
    up_rank_factor = jnp.dot(tokens, new_in_hidden[1], preferred_element_type=jnp.float32).astype(jnp.bfloat16)
    sig = jax.nn.sigmoid(gate)
    hidden = (gate * sig * up).astype(jnp.bfloat16)
    down_rank_factor = jnp.dot(hidden, new_in_down, preferred_element_type=jnp.float32).astype(jnp.bfloat16)
    hidden_grad = lax.dot_general(cotangent, merged_down, (((1,), (1,)), ((), ())), preferred_element_type=jnp.float32)
    gate_branch_gradient = (hidden_grad * up * sig * (1.0 + gate * (1.0 - sig))).astype(jnp.bfloat16)
    up_branch_gradient = (hidden_grad * gate * sig).astype(jnp.bfloat16)
    input_grad = (lax.dot_general(gate_branch_gradient, merged_gate, (((1,), (1,)), ((), ())), preferred_element_type=jnp.float32)
                  + lax.dot_general(up_branch_gradient, merged_up, (((1,), (1,)), ((), ())), preferred_element_type=jnp.float32)).astype(jnp.bfloat16)
    gate_adapter_gradient = adapter_scale * lax.dot_general(gate_rank_factor, gate_branch_gradient, (((0,), (0,)), ((), ())), preferred_element_type=jnp.float32)
    up_adapter_gradient = adapter_scale * lax.dot_general(up_rank_factor, up_branch_gradient, (((0,), (0,)), ((), ())), preferred_element_type=jnp.float32)
    grad_hidden = jnp.stack([gate_adapter_gradient, up_adapter_gradient])
    down_adapter_gradient = adapter_scale * lax.dot_general(down_rank_factor, cotangent, (((0,), (0,)), ((), ())), preferred_element_type=jnp.float32)
    keep_h = keep_hidden.astype(jnp.float32)[:, None, :]
    keep_d = keep_down.astype(jnp.float32)[None, :]
    new_first_hidden = 0.9 * keep_h * first_hidden + 0.1 * grad_hidden
    new_second_hidden = 0.999 * keep_h * second_hidden + 0.001 * grad_hidden * grad_hidden
    new_first_down = 0.9 * keep_d * first_down + 0.1 * down_adapter_gradient
    new_second_down = 0.999 * keep_d * second_down + 0.001 * down_adapter_gradient * down_adapter_gradient
    return input_grad, new_first_hidden, new_second_hidden, new_first_down, new_second_down
```

```python
from types import SimpleNamespace

import jax
import jax.numpy as jnp
from jax import lax
from jax.experimental import pallas as pl
from jax.experimental.pallas import tpu as pltpu
from jax.sharding import PartitionSpec as P

MESH = pl.DeviceIdType.MESH
F32 = jnp.float32
BF16 = jnp.bfloat16
SCALE = 0.25
OWNED = ((0, 3), (1, 2))
OFFSET = (0, 1, 3, 2)
SLOT = {o: q for q, o in enumerate(OFFSET)}
OWNER = {q: (k, s) for k, qs in enumerate(OWNED) for s, q in enumerate(qs)}


def dot(a, b):
    return lax.dot_general(a, b, (((1,), (0,)), ((), ())), preferred_element_type=F32)


def dot_t(a, b):
    return lax.dot_general(a, b, (((1,), (1,)), ((), ())), preferred_element_type=F32)


def one_hot(rows, cols, source):
    i = lax.broadcasted_iota(jnp.int32, (rows, cols), 0)
    j = lax.broadcasted_iota(jnp.int32, (rows, cols), 1)
    return jnp.where(source(i, j), 1.0, 0.0).astype(BF16)


SCRATCH = dict(
    w_hidden=((1024, 1024), BF16),
    w_down=((512, 1024), BF16),
    new_down_t=((4, 128, 128), BF16),
    units=((4, 16, 1024), BF16),
    quads=((4, 40, 1024), BF16),
    strip=((40, 384), BF16),
    strips=((2, 4, 40, 384), BF16),
    far_quads=((4, 40, 1024), BF16),
    left=((4, 160, 640), BF16),
    right=((4, 160, 384), BF16),
    part_send=((4, 80, 1536), BF16),
    part_recv=((4, 80, 1536), BF16),
    part=((2, 12, 80, 128), F32),
    part_b=((2, 12, 80, 128), BF16),
    relay_recv=((2, 3, 80, 128), BF16),
    relay_send=((2, 3, 80, 128), BF16),
    near_recv=((2, 3, 80, 128), BF16),
    far_recv=((2, 3, 80, 128), BF16),
    grads=((4, 4, 2, 80, 128), BF16),
    hid=((2, 80, 128), BF16),
    xy_send=((4, 4, 24, 1024), BF16),
    xy_recv=((4, 4, 24, 1024), BF16),
    z_own=((4, 8, 1024), F32),
    z_send=((4, 8, 1024), BF16),
    z_recv=((4, 8, 1024), BF16),
    d_part=((4, 32, 256), F32),
    d_xrecv=((4, 32, 256), F32),
    d_sum=((4, 8, 256), F32),
    d_zrecv=((4, 8, 256), F32),
    d_col=((8, 256), F32),
    d_crecv=((4, 8, 256), F32),
    d_both=((4, 2, 8, 256), F32),
    lt_f=((2, 4, 32, 128), F32),
    lt_b=((2, 4, 32, 128), BF16),
    lt_crecv=((4, 32, 128), BF16),
    lt_two=((4, 32, 128), F32),
    lt_two_b=((4, 32, 128), BF16),
    lt_zrecv=((4, 32, 128), BF16),
    lt=((4, 32, 128), BF16),
)
INPUTS = dict(
    tokens=(5, 1024), cotangent=(5, 1024), gate_raw=(448, 1024), up_raw=(448, 1024), down_raw=(448, 1024),
    in_raw=(2, 1024, 128), out_hidden=(2, 448, 128), in_down=(448, 128), out_down=(128, 1024),
    new_in=(2, 1024, 128), new_down=(448, 128),
)
N_SEM = 112


def kernel(*refs):
    n_in = len(INPUTS)
    ig_out, gh_out, gd_out = refs[n_in : n_in + 3]
    far = SimpleNamespace(**dict(zip(INPUTS, refs[:n_in])))
    inner = refs[n_in + 3 :]
    r = SimpleNamespace(**dict(zip(list(INPUTS) + list(SCRATCH), inner)))
    send_sem, recv_sem, local_sem = inner[n_in + len(SCRATCH) :]

    row, col = lax.axis_index("row"), lax.axis_index("col")
    x, zl, y = row // 16, lax.rem(row // 4, 4), lax.rem(row, 4)
    zh, k = col // 2, lax.rem(col, 2)

    def at(dx=0, dz=0, dy=0, dh=0, flip=False):
        to_row = lax.rem(x + dx, 4) * 16 + lax.rem(zl + dz, 4) * 4 + lax.rem(y + dy, 4)
        return (to_row, lax.rem(zh + dh, 4) * 2 + (1 - k if flip else k))

    peers = [at(dx=d) for d in (1, 2, 3)] + [at(dz=d) for d in (1, 2, 3)]
    peers += [at(dx=d, dy=e) for d in range(4) for e in (1, 2, 3)] + [at(dh=d) for d in (1, 2, 3)] + [at(flip=True)]
    barrier = pltpu.get_barrier_semaphore()
    for peer in peers:
        pl.semaphore_signal(barrier, inc=1, device_id=peer, device_id_type=MESH)

    loads = SimpleNamespace()
    for n, (name, ref) in enumerate(vars(far).items()):
        copy = pltpu.make_async_copy(ref, vars(r)[name], local_sem.at[n])
        copy.start()
        vars(loads)[name] = copy

    ids = []

    def send(src, dst, to):
        n = len(ids)
        ids.append(n)
        return pltpu.make_async_remote_copy(
            src_ref=src, dst_ref=dst, send_sem=send_sem.at[n], recv_sem=recv_sem.at[n], device_id=to, device_id_type=MESH
        )

    units = r.units
    units[zl] = jnp.zeros((16, 1024), BF16)
    loads.tokens.wait()
    loads.cotangent.wait()
    units[zl, pl.ds(0, 5), :] = r.tokens[...]
    units[zl, pl.ds(8, 5), :] = r.cotangent[...]
    pl.semaphore_wait(barrier, len(peers))
    first = [send(units.at[zl], units.at[zl], at(dz=d)) for d in (1, 2, 3)]
    for copy in first:
        copy.start()

    for copy in list(vars(loads).values())[2:]:
        copy.wait()
    w_hidden, w_down = r.w_hidden, r.w_down

    def merge_rows(n, _):
        rows = pl.ds(pl.multiple_of(n * 224, 224), 224)
        for b, raw in enumerate((r.gate_raw, r.up_raw)):
            step = dot_t(r.out_hidden[b, rows, :], r.in_raw[b])
            to = pl.ds(pl.multiple_of(b * 512 + n * 224, 32), 224)
            w_hidden[to, :] = (raw[rows, :].astype(F32) + SCALE * step).astype(BF16)
        step = dot(r.in_down[rows, :], r.out_down[...])
        w_down[rows, :] = (r.down_raw[rows, :].astype(F32) + SCALE * step).astype(BF16)
        return 0

    lax.fori_loop(0, 2, merge_rows, 0)
    for n in range(2):
        w_hidden[n * 512 + 448 : n * 512 + 512, :] = jnp.zeros((64, 1024), BF16)
    w_down[448:512, :] = jnp.zeros((64, 1024), BF16)
    for j in range(3):
        r.new_down_t[j] = r.new_down[128 * j : 128 * j + 128, :].astype(F32).T.astype(BF16)
    last = jnp.concatenate([r.new_down[384:448, :].astype(F32), jnp.zeros((64, 128), F32)], axis=0)
    r.new_down_t[3] = last.T.astype(BF16)

    for copy in first:
        copy.wait_recv()
    pick = one_hot(40, 64, lambda i, j: ((j & 7) < 5) & (i == ((j >> 3) & 1) * 20 + (j >> 4) * 5 + (j & 7)))
    quads, strip, strips, far_quads = r.quads, r.strip, r.strips, r.far_quads
    left, right = r.left, r.right
    quad = dot(pick, units[...].reshape(64, 1024)).astype(BF16)
    quads[x] = quad
    strip[...] = quad[:, 640:]
    second = [send(quads.at[x], quads.at[x], at(dx=d)) for d in (1, 2, 3)]
    over_y = [send(strip, strips.at[0, x], at(dy=3)), send(strip, strips.at[1, x], at(dy=1))]
    over_y += [send(quads.at[x], far_quads.at[x], at(dy=2))]
    for copy in second + over_y:
        copy.start()

    def arrange(get):
        total = None
        for n in range(4):
            place = one_hot(160, 40, lambda i, j, n=n: i == n * 20 + j + jnp.where(j >= 20, 60, 0))
            term = dot(place, get(n))
            total = term if total is None else total + term
        return total.astype(BF16)

    for copy in second:
        copy.wait_recv()
    chunk = arrange(lambda n: quads[n])
    left[0] = chunk[:, :640]
    right[0] = chunk[:, 640:]

    to_up = send(left.at[0], left.at[2], at(dy=1))
    to_down = send(left.at[0], left.at[1], at(dy=3))
    over_x = {
        q: [send(ref.at[x], ref.at[x], at(dx=d)) for d in (1, 2, 3)]
        for q, ref in ((1, strips.at[0]), (2, strips.at[1]), (3, far_quads))
    }
    to_up.start()
    to_down.start()
    for q in (1, 2, 3):
        over_y[q - 1].wait_recv()
        for copy in over_x[q]:
            copy.start()

    def build(q):
        if q < 3:
            (to_down, to_up)[q - 1].wait_recv()
        for copy in over_x[q]:
            copy.wait_recv()
        if q < 3:
            right[q] = arrange(lambda n: strips[q - 1, n])
        else:
            chunk = arrange(lambda n: far_quads[n])
            left[q] = chunk[:, :640]
            right[q] = chunk[:, 640:]

    def tokens(q):
        return jnp.concatenate([left[q, 0:80, :], right[q, 0:80, :]], axis=1)

    def cotangent(q):
        return jnp.concatenate([left[q, 80:160, :], right[q, 80:160, :]], axis=1)

    partner = at(flip=True)
    part_copy = {q: send(r.part_send.at[q], r.part_recv.at[q], partner) for q in range(4)}
    grads = r.grads
    grad_copy = {q: send(grads.at[q], grads.at[q], partner) for q in range(4)}
    xy_copy = {
        q: [
            send(r.xy_send.at[q, lax.rem(x + d, 4)], r.xy_recv.at[q, d], at(dx=d, dy=OFFSET[q]))
            for d in range(4)
            if q or d
        ]
        for q in range(4)
    }

    def products(q):
        for n in range(2):
            yield n * 4, dot_t(tokens(q), w_hidden[n * 512 : n * 512 + 512, :])
        yield 8, dot_t(cotangent(q), w_down[...])

    def give(q):
        for block, value in products(q):
            r.part_send[q, :, block * 128 : block * 128 + 512] = value.astype(BF16)
        part_copy[q].start()

    def keep(q):
        s = OWNER[q][1]
        for block, value in products(q):
            for b in range(4):
                r.part[s, b * 3 + block // 4] = value[:, b * 128 : b * 128 + 128]

    def groups(q):
        return ((0, 2), (2, 1)) if q in (0, 2) else ((2, 1), (0, 2))

    def ring(q):
        s = OWNER[q][1]
        (a0, an), (b0, bn) = groups(q)

        def at_j(ref, d, lo, n):
            return ref.at[s, pl.ds(lax.rem(zh + d, 4) * 3 + lo, n)]

        half = lambda ref, lo, n: ref.at[s, pl.ds(lo, n)]
        mine = r.part_b
        return SimpleNamespace(
            far_a=send(at_j(mine, 2, a0, an), half(r.relay_recv, a0, an), at(dh=1)),
            near_b=send(at_j(mine, 1, b0, bn), half(r.near_recv, b0, bn), at(dh=1)),
            far_b=send(at_j(mine, 2, b0, bn), half(r.relay_recv, b0, bn), at(dh=3)),
            near_a=send(at_j(mine, 3, a0, an), half(r.near_recv, a0, an), at(dh=3)),
            on_a=send(half(r.relay_send, a0, an), half(r.far_recv, a0, an), at(dh=1)),
            on_b=send(half(r.relay_send, b0, bn), half(r.far_recv, b0, bn), at(dh=3)),
        )

    rings = {q: ring(q) for q in range(4)}

    def reduce_start(q):
        s = OWNER[q][1]
        part_copy[q].wait_recv()
        for b in range(4):
            for c in range(3):
                lanes = c * 512 + b * 128
                total = r.part[s, b * 3 + c] + r.part_recv[q, :, lanes : lanes + 128].astype(F32)
                r.part[s, b * 3 + c] = total
                r.part_b[s, b * 3 + c] = total.astype(BF16)
        for copy in (rings[q].far_a, rings[q].far_b, rings[q].near_b, rings[q].near_a):
            copy.start()

    def reduce_relay(q):
        s = OWNER[q][1]
        for (lo, n), d, far, on in (
            (groups(q)[0], 1, rings[q].far_a, rings[q].on_a),
            (groups(q)[1], 3, rings[q].far_b, rings[q].on_b),
        ):
            far.wait_recv()
            base = lax.rem(zh + d, 4) * 3
            for c in range(lo, lo + n):
                total = r.part[s, base + c] + r.relay_recv[s, c].astype(F32)
                r.relay_send[s, c] = total.astype(BF16)
            on.start()

    def gather(q):
        here, low, high = zh, lax.rem(zh + 3, 4), lax.rem(zh + 1, 4)
        return SimpleNamespace(
            up=send(grads.at[q, here], grads.at[q, here], at(dh=1)),
            down=send(grads.at[q, here], grads.at[q, here], at(dh=3)),
            on_up=send(grads.at[q, low, pl.ds(0, 1)], grads.at[q, low, pl.ds(0, 1)], at(dh=1)),
            on_down=send(grads.at[q, high, pl.ds(1, 1)], grads.at[q, high, pl.ds(1, 1)], at(dh=3)),
        )

    gathers = {q: gather(q) for q in range(4)}

    def activate(q):
        s = OWNER[q][1]
        for copy in (rings[q].near_a, rings[q].near_b, rings[q].on_a, rings[q].on_b):
            copy.wait_recv()
        gate, up, hidden_grad = (
            r.part[s, zh * 3 + c] + r.near_recv[s, c].astype(F32) + r.far_recv[s, c].astype(F32) for c in range(3)
        )
        sig = jax.nn.sigmoid(gate)
        grads[q, zh, 0] = (hidden_grad * up * sig * (1.0 + gate * (1.0 - sig))).astype(BF16)
        grads[q, zh, 1] = (hidden_grad * gate * sig).astype(BF16)
        gathers[q].up.start()
        gathers[q].down.start()
        r.hid[s] = (gate * sig * up).astype(BF16)

    def gather_relay(q):
        gathers[q].up.wait_recv()
        gathers[q].on_up.start()
        gathers[q].down.wait_recv()
        gathers[q].on_down.start()

    def gather_end(q):
        gathers[q].on_up.wait_recv()
        gathers[q].on_down.wait_recv()
        grad_copy[q].start()

    def both(q):
        return jnp.concatenate([grads[q, j, c] for c in range(2) for j in range(4)], axis=1)

    def backward(q):
        both_grads = both(q)

        def source(i, j):
            part = jnp.where(i >= 24, 1, 0) + jnp.where(i >= 48, 1, 0) + jnp.where(i >= 72, 1, 0)
            inside = i - 24 * part
            return (inside < 20) & (j == part * 20 + inside)

        spread = one_hot(96, 80, source)
        for n in range(2):
            value = dot(both_grads, w_hidden[:, n * 512 : n * 512 + 512]).astype(BF16)
            wide = dot(spread, value).astype(BF16)
            for m in range(4):
                r.xy_send[q, m, :, n * 512 : n * 512 + 512] = wide[24 * m : 24 * m + 24]
        for copy in xy_copy[q]:
            copy.start()

    def take(q):
        grad_copy[q].wait_recv()
        backward(q)

    lt_core = send(r.lt_b.at[1 - k], r.lt_crecv, partner)
    lt_z = [send(r.lt_two_b.at[lax.rem(zh + d, 4)], r.lt_zrecv.at[d], at(dh=d)) for d in (1, 2, 3)]
    lt_y = [send(r.lt.at[0], r.lt.at[q], at(dy=(4 - OFFSET[q]) % 4)) for q in (1, 2, 3)]

    def low_start():
        for b in range(2):
            low = dot(tokens(0), r.new_in[b])
            low = jnp.concatenate([low, jnp.zeros((48, 128), F32)], axis=0).T
            for c in range(8):
                value = low[16 * c : 16 * c + 16, :]
                r.lt_f[c % 2, c // 2, 16 * b : 16 * b + 16, :] = value
                r.lt_b[c % 2, c // 2, 16 * b : 16 * b + 16, :] = value.astype(BF16)
        lt_core.start()

    def low_middle():
        lt_core.wait_recv()
        total = r.lt_f[k] + r.lt_crecv[...].astype(F32)
        r.lt_two[...] = total
        r.lt_two_b[...] = total.astype(BF16)
        for copy in lt_z:
            copy.start()

    def low_end():
        total = r.lt_two[zh]
        for d, copy in zip((1, 2, 3), lt_z):
            copy.wait_recv()
            total += r.lt_zrecv[d].astype(F32)
        r.lt[0] = total.astype(BF16)
        for copy in lt_y:
            copy.start()

    d_x = [send(r.d_part.at[lax.rem(x + d, 4)], r.d_xrecv.at[d], at(dx=d)) for d in (1, 2, 3)]
    d_z = [send(r.d_sum.at[lax.rem(zl + d, 4)], r.d_zrecv.at[d], at(dz=d)) for d in (1, 2, 3)]
    d_h = [send(r.d_col, r.d_crecv.at[d], at(dh=d)) for d in (1, 2, 3)]
    d_k = send(r.d_both.at[0, k], r.d_both.at[0, k], partner)
    d_y = [send(r.d_both.at[0], r.d_both.at[d], at(dy=4 - d)) for d in (1, 2, 3)]

    def down_x():
        for s in range(2):
            value = dot_t(r.new_down_t[zh], r.hid[s])
            value = jnp.concatenate([value, jnp.zeros((128, 48), F32)], axis=1)
            for n in range(4):
                r.d_part[n, :, s * 128 : s * 128 + 128] = value[32 * n : 32 * n + 32]
        for copy in d_x:
            copy.start()

    def down_z():
        total = r.d_part[x]
        for d, copy in zip((1, 2, 3), d_x):
            copy.wait_recv()
            total += r.d_xrecv[d]
        for n in range(4):
            r.d_sum[n] = total[8 * n : 8 * n + 8]
        for copy in d_z:
            copy.start()

    def down_h():
        total = r.d_sum[zl]
        for d, copy in zip((1, 2, 3), d_z):
            copy.wait_recv()
            total += r.d_zrecv[d]
        r.d_col[...] = total
        for copy in d_h:
            copy.start()

    def down_k():
        total = r.d_col[...]
        for d, copy in zip((1, 2, 3), d_h):
            copy.wait_recv()
            total += r.d_crecv[d]
        r.d_both[0, k] = total
        d_k.start()

    def down_y():
        d_k.wait_recv()
        for copy in d_y:
            copy.start()

    def down_end():
        for copy in d_y:
            copy.wait_recv()
        out = None
        for q in range(4):
            total = None
            for d in range(4):
                core, s = OWNER[SLOT[(OFFSET[q] - d) % 4]]
                term = r.d_both[d, core, :, s * 128 : s * 128 + 128]
                total = term if total is None else total + term
            term = dot(total[:, 0:80].astype(BF16), cotangent(q))
            out = term if out is None else out + term
        mine = out[0:2]
        for n in (1, 2, 3):
            mine = jnp.where(y == n, out[2 * n : 2 * n + 2], mine)
        gd_out[...] = SCALE * mine

    orders = (
        (
            (keep, 0), (reduce_start, 0), (low_start,), (build, 1), (give, 1), (build, 2), (give, 2), (build, 3),
            (keep, 3), (reduce_start, 3), (reduce_relay, 0), (low_middle,), (activate, 0), (reduce_relay, 3),
            (gather_relay, 0), (low_end,), (gather_end, 0), (backward, 0), (activate, 3), (down_x,), (take, 1),
            (gather_relay, 3), (down_z,), (take, 2), (gather_end, 3), (backward, 3),
        ),
        (
            (give, 0), (low_start,), (build, 1), (keep, 1), (reduce_start, 1), (build, 2), (keep, 2),
            (reduce_start, 2), (build, 3), (give, 3), (low_middle,), (reduce_relay, 1), (reduce_relay, 2),
            (activate, 1), (activate, 2), (down_x,), (low_end,), (gather_relay, 1), (gather_relay, 2), (take, 0),
            (gather_end, 1), (backward, 1), (gather_end, 2), (backward, 2), (down_z,), (take, 3),
        ),
    )
    for core in range(2):

        @pl.when(k == core)
        def _():
            for step, *args in orders[core]:
                step(*args)

    def flush(copies):
        for copy in copies:
            copy.wait_send()

    down_h()
    flush(first + second + over_y + [to_up, to_down, lt_core] + over_x[1] + over_x[2] + over_x[3] + lt_z)
    for copy in lt_y:
        copy.wait_recv()
    for b in range(2):
        out = None
        for q in range(4):
            columns = jnp.concatenate([grads[q, j, b] for j in range(4)], axis=1)
            term = dot(r.lt[q, 16 * b : 16 * b + 16, 0:80], columns)
            out = term if out is None else out + term
        gh_out[b] = SCALE * out[:, 0:448]
    for core in range(2):

        @pl.when(k == core)
        def _():
            for q in OWNED[core]:
                flush(list(vars(rings[q]).values()) + list(vars(gathers[q]).values()) + [grad_copy[q]])
            flush([part_copy[q] for q in OWNED[1 - core]])

    flush(d_x + d_z + lt_y)
    down_k()
    total = r.xy_send[0, x].astype(F32)
    for q in (0, 1, 2, 3):
        if q == 3:
            down_y()
        for copy in xy_copy[q]:
            copy.wait_recv()
        for d in range(4):
            if q or d:
                total += r.xy_recv[q, d].astype(F32)
    spread = one_hot(32, 24, lambda i, j: ((i & 7) < 5) & (j == (i >> 3) * 5 + (i & 7)))
    wide = dot(spread, total.astype(BF16))
    for n in range(4):
        r.z_own[n] = wide[8 * n : 8 * n + 8]
        r.z_send[n] = wide[8 * n : 8 * n + 8].astype(BF16)
    z_copies = [send(r.z_send.at[lax.rem(zl + d, 4)], r.z_recv.at[d], at(dz=d)) for d in (1, 2, 3)]
    for copy in z_copies:
        copy.start()
    flush(d_h + [d_k] + d_y + xy_copy[0] + xy_copy[1] + xy_copy[2] + xy_copy[3])
    down_end()
    total = r.z_own[zl]
    for d, copy in zip((1, 2, 3), z_copies):
        copy.wait_recv()
        total += r.z_recv[d].astype(F32)
    ig_out[...] = total.astype(BF16)
    flush(z_copies)


def moments(*refs):
    ins, outs, ins_v, outs_v = refs[:9], refs[9:14], refs[14:23], refs[23:28]
    in_sem, out_sem = refs[28:]
    loads = [pltpu.make_async_copy(a, b, in_sem.at[n]) for n, (a, b) in enumerate(zip(ins, ins_v))]
    stores = [pltpu.make_async_copy(a, b, out_sem.at[n]) for n, (a, b) in enumerate(zip(outs_v, outs))]
    for copy in loads:
        copy.start()
    for copy in loads:
        copy.wait()
    ig, grad_hidden, grad_down, first_hidden, second_hidden, first_down, second_down, keep_hidden, keep_down = ins_v
    outs_v[0][...] = ig[0:5, :]
    stores[0].start()
    keep = keep_hidden[...].astype(F32)
    for n in range(2):
        kept = jnp.broadcast_to(keep[n : n + 1, :], (16, 448))
        grad = grad_hidden[n]
        outs_v[1][n] = 0.9 * kept * first_hidden[n] + 0.1 * grad
        outs_v[2][n] = 0.999 * kept * second_hidden[n] + 0.001 * grad * grad
    stores[1].start()
    stores[2].start()
    kept = jnp.broadcast_to(keep_down[...].astype(F32), (2, 1024))
    grad = grad_down[...]
    outs_v[3][...] = 0.9 * kept * first_down[...] + 0.1 * grad
    outs_v[4][...] = 0.999 * kept * second_down[...] + 0.001 * grad * grad
    stores[3].start()
    stores[4].start()
    for copy in stores:
        copy.wait()


def body(
    tokens, cotangent, gate_weight, up_weight, down_weight, old_in_hidden, old_out_hidden, old_in_down,
    old_out_down, new_in_hidden, new_in_down, first_hidden, second_hidden, first_down, second_down,
    keep_hidden, keep_down,
):
    vmem = pl.BlockSpec(memory_space=pltpu.VMEM)
    far = pl.BlockSpec(memory_space=pltpu.HBM)
    ig, grad_hidden, grad_down = pl.pallas_call(
        kernel,
        out_shape=(
            jax.ShapeDtypeStruct((8, 1024), BF16),
            jax.ShapeDtypeStruct((2, 16, 448), F32),
            jax.ShapeDtypeStruct((2, 1024), F32),
        ),
        in_specs=[far] * len(INPUTS),
        out_specs=(vmem, vmem, vmem),
        scratch_shapes=[pltpu.VMEM(shape, BF16) for shape in INPUTS.values()]
        + [pltpu.VMEM(*spec) for spec in SCRATCH.values()]
        + [pltpu.SemaphoreType.DMA((N_SEM,)), pltpu.SemaphoreType.DMA((N_SEM,)), pltpu.SemaphoreType.DMA((len(INPUTS),))],
        compiler_params=pltpu.CompilerParams(
            collective_id=0, has_side_effects=True, vmem_limit_bytes=63 * 2**20
        ),
        cost_estimate=pl.CostEstimate(flops=2_000_000_000, bytes_accessed=4_000_000, transcendentals=150_000),
        name="layer",
    )(
        tokens, cotangent, gate_weight.T, up_weight.T, down_weight, old_in_hidden, old_out_hidden.transpose(0, 2, 1),
        old_in_down, old_out_down, new_in_hidden, new_in_down,
    )
    sources = (
        ig, grad_hidden, grad_down, first_hidden, second_hidden, first_down, second_down, keep_hidden,
        keep_down.reshape(1, 1024),
    )
    results = (
        jax.ShapeDtypeStruct((5, 1024), BF16),
        jax.ShapeDtypeStruct((2, 16, 448), F32),
        jax.ShapeDtypeStruct((2, 16, 448), F32),
        jax.ShapeDtypeStruct((2, 1024), F32),
        jax.ShapeDtypeStruct((2, 1024), F32),
    )
    return pl.pallas_call(
        moments,
        out_shape=results,
        in_specs=[far] * len(sources),
        out_specs=[far] * len(results),
        scratch_shapes=[pltpu.VMEM(a.shape, a.dtype) for a in sources + results]
        + [pltpu.SemaphoreType.DMA((len(sources),)), pltpu.SemaphoreType.DMA((len(results),))],
        compiler_params=pltpu.CompilerParams(vmem_limit_bytes=63 * 2**20),
        name="moments",
    )(*sources)


def solution(mesh):
    return jax.shard_map(
        body,
        mesh=mesh,
        in_specs=(
            P("row", "col"), P("row", "col"), P("col", "row"), P("col", "row"), P("row", "col"),
            P(None, "col", None), P(None, None, "row"), P("row", None), P(None, "col"), P(None, "col", None),
            P("row", None), P(None, "col", "row"), P(None, "col", "row"), P("row", "col"), P("row", "col"),
            P(None, "row"), P("col"),
        ),
        out_specs=(
            P("row", "col"), P(None, "col", "row"), P(None, "col", "row"), P("row", "col"), P("row", "col"),
        ),
        check_vma=False,
    )
```

```python
from types import SimpleNamespace

import jax
import jax.numpy as jnp
from jax import lax
from jax.experimental import pallas as pl
from jax.experimental.pallas import tpu as pltpu
from jax.sharding import PartitionSpec as P

MESH = pl.DeviceIdType.MESH
F32 = jnp.float32
BF16 = jnp.bfloat16
SCALE = 0.25
OWNED = ((0, 3), (1, 2))
OFFSET = (0, 1, 3, 2)
SLOT = {o: q for q, o in enumerate(OFFSET)}
OWNER = {q: (k, s) for k, qs in enumerate(OWNED) for s, q in enumerate(qs)}


def dot(a, b):
    return lax.dot_general(a, b, (((1,), (0,)), ((), ())), preferred_element_type=F32)


def dot_t(a, b):
    return lax.dot_general(a, b, (((1,), (1,)), ((), ())), preferred_element_type=F32)


def one_hot(rows, cols, source):
    i = lax.broadcasted_iota(jnp.int32, (rows, cols), 0)
    j = lax.broadcasted_iota(jnp.int32, (rows, cols), 1)
    return jnp.where(source(i, j), 1.0, 0.0).astype(BF16)


SCRATCH = dict(
    w_hidden=((1024, 1024), BF16),
    w_down=((512, 1024), BF16),
    new_down_t=((4, 128, 128), BF16),
    units=((4, 16, 1024), BF16),
    quads=((4, 40, 1024), BF16),
    strip=((40, 512), BF16),
    strips=((2, 4, 40, 512), BF16),
    far_quads=((4, 40, 1024), BF16),
    left=((4, 160, 512), BF16),
    right=((4, 160, 512), BF16),
    part_send=((4, 80, 1536), BF16),
    part_recv=((4, 80, 1536), BF16),
    part=((2, 12, 80, 128), F32),
    part_b=((2, 12, 80, 128), BF16),
    relay_recv=((2, 3, 80, 128), BF16),
    relay_send=((2, 3, 80, 128), BF16),
    near_recv=((2, 3, 80, 128), BF16),
    far_recv=((2, 3, 80, 128), BF16),
    grads=((4, 4, 2, 80, 128), BF16),
    hid=((2, 80, 128), BF16),
    xy_send=((4, 4, 24, 1024), BF16),
    xy_recv=((4, 4, 24, 1024), BF16),
    z_own=((4, 8, 1024), F32),
    z_send=((4, 8, 1024), BF16),
    z_recv=((4, 8, 1024), BF16),
    d_part=((4, 32, 256), F32),
    d_xrecv=((4, 32, 256), F32),
    d_sum=((4, 8, 256), F32),
    d_zrecv=((4, 8, 256), F32),
    d_col=((8, 256), F32),
    d_crecv=((4, 8, 256), F32),
    d_both=((4, 2, 8, 256), F32),
    lt_f=((2, 4, 32, 128), F32),
    lt_b=((2, 4, 32, 128), BF16),
    lt_crecv=((4, 32, 128), BF16),
    lt_two=((4, 2, 16, 128), F32),
    lt_two_b=((4, 2, 16, 128), BF16),
    lt_relay_recv=((2, 16, 128), BF16),
    lt_relay_send=((2, 16, 128), BF16),
    lt_near=((2, 16, 128), BF16),
    lt_far=((2, 16, 128), BF16),
    lt=((4, 32, 128), BF16),
)
INPUTS = dict(
    tokens=(5, 1024), cotangent=(5, 1024), gate_raw=(448, 1024), up_raw=(448, 1024), down_raw=(448, 1024),
    in_raw=(2, 1024, 128), out_hidden=(2, 448, 128), in_down=(448, 128), out_down=(128, 1024),
    new_in=(2, 1024, 128), new_down=(448, 128),
)
N_SEM = 112


def kernel(*refs):
    n_in = len(INPUTS)
    ig_out, gh_out, gd_out = refs[n_in : n_in + 3]
    far = SimpleNamespace(**dict(zip(INPUTS, refs[:n_in])))
    inner = refs[n_in + 3 :]
    r = SimpleNamespace(**dict(zip(list(INPUTS) + list(SCRATCH), inner)))
    send_sem, recv_sem, local_sem = inner[n_in + len(SCRATCH) :]

    row, col = lax.axis_index("row"), lax.axis_index("col")
    x, zl, y = row // 16, lax.rem(row // 4, 4), lax.rem(row, 4)
    zh, k = col // 2, lax.rem(col, 2)

    def at(dx=0, dz=0, dy=0, dh=0, flip=False):
        to_row = lax.rem(x + dx, 4) * 16 + lax.rem(zl + dz, 4) * 4 + lax.rem(y + dy, 4)
        return (to_row, lax.rem(zh + dh, 4) * 2 + (1 - k if flip else k))

    peers = [at(dx=d) for d in (1, 2, 3)] + [at(dz=d) for d in (1, 2, 3)]
    peers += [at(dx=d, dy=e) for d in range(4) for e in (1, 2, 3)] + [at(dh=d) for d in (1, 3)] + [at(flip=True)]
    barrier = pltpu.get_barrier_semaphore()
    for peer in peers:
        pl.semaphore_signal(barrier, inc=1, device_id=peer, device_id_type=MESH)

    loads = SimpleNamespace()
    for n, (name, ref) in enumerate(vars(far).items()):
        copy = pltpu.make_async_copy(ref, vars(r)[name], local_sem.at[n])
        copy.start()
        vars(loads)[name] = copy

    ids = []

    def send(src, dst, to):
        n = len(ids)
        ids.append(n)
        return pltpu.make_async_remote_copy(
            src_ref=src, dst_ref=dst, send_sem=send_sem.at[n], recv_sem=recv_sem.at[n], device_id=to, device_id_type=MESH
        )

    units = r.units
    units[zl] = jnp.zeros((16, 1024), BF16)
    loads.tokens.wait()
    loads.cotangent.wait()
    units[zl, pl.ds(0, 5), :] = r.tokens[...]
    units[zl, pl.ds(8, 5), :] = r.cotangent[...]
    pl.semaphore_wait(barrier, len(peers))
    first = [send(units.at[zl], units.at[zl], at(dz=d)) for d in (1, 2, 3)]
    for copy in first:
        copy.start()

    for copy in list(vars(loads).values())[2:]:
        copy.wait()
    w_hidden, w_down = r.w_hidden, r.w_down

    def merge_rows(n, _):
        rows = pl.ds(pl.multiple_of(n * 224, 224), 224)
        for b, raw in enumerate((r.gate_raw, r.up_raw)):
            step = dot_t(r.out_hidden[b, rows, :], r.in_raw[b])
            to = pl.ds(pl.multiple_of(b * 512 + n * 224, 32), 224)
            w_hidden[to, :] = (raw[rows, :].astype(F32) + SCALE * step).astype(BF16)
        step = dot(r.in_down[rows, :], r.out_down[...])
        w_down[rows, :] = (r.down_raw[rows, :].astype(F32) + SCALE * step).astype(BF16)
        return 0

    lax.fori_loop(0, 2, merge_rows, 0)
    for n in range(2):
        w_hidden[n * 512 + 448 : n * 512 + 512, :] = jnp.zeros((64, 1024), BF16)
    w_down[448:512, :] = jnp.zeros((64, 1024), BF16)
    for j in range(3):
        r.new_down_t[j] = r.new_down[128 * j : 128 * j + 128, :].astype(F32).T.astype(BF16)
    last = jnp.concatenate([r.new_down[384:448, :].astype(F32), jnp.zeros((64, 128), F32)], axis=0)
    r.new_down_t[3] = last.T.astype(BF16)

    for copy in first:
        copy.wait_recv()
    pick = one_hot(40, 64, lambda i, j: ((j & 7) < 5) & (i == ((j >> 3) & 1) * 20 + (j >> 4) * 5 + (j & 7)))
    quads, strip, strips, far_quads = r.quads, r.strip, r.strips, r.far_quads
    left, right = r.left, r.right
    quad = dot(pick, units[...].reshape(64, 1024)).astype(BF16)
    quads[x] = quad
    strip[...] = quad[:, 512:]
    second = [send(quads.at[x], quads.at[x], at(dx=d)) for d in (1, 2, 3)]
    over_y = [send(strip, strips.at[0, x], at(dy=3)), send(strip, strips.at[1, x], at(dy=1))]
    over_y += [send(quads.at[x], far_quads.at[x], at(dy=2))]
    for copy in second + over_y:
        copy.start()

    def arrange(get):
        total = None
        for n in range(4):
            place = one_hot(160, 40, lambda i, j, n=n: i == n * 20 + j + jnp.where(j >= 20, 60, 0))
            term = dot(place, get(n))
            total = term if total is None else total + term
        return total.astype(BF16)

    for copy in second:
        copy.wait_recv()
    chunk = arrange(lambda n: quads[n])
    left[0] = chunk[:, :512]
    right[0] = chunk[:, 512:]

    to_up = send(left.at[0], left.at[2], at(dy=1))
    to_down = send(left.at[0], left.at[1], at(dy=3))
    over_x = {
        q: [send(ref.at[x], ref.at[x], at(dx=d)) for d in (1, 2, 3)]
        for q, ref in ((1, strips.at[0]), (2, strips.at[1]), (3, far_quads))
    }
    to_up.start()
    to_down.start()
    for q in (1, 2, 3):
        over_y[q - 1].wait_recv()
        for copy in over_x[q]:
            copy.start()

    def build(q):
        if q < 3:
            (to_down, to_up)[q - 1].wait_recv()
        for copy in over_x[q]:
            copy.wait_recv()
        if q < 3:
            right[q] = arrange(lambda n: strips[q - 1, n])
        else:
            chunk = arrange(lambda n: far_quads[n])
            left[q] = chunk[:, :512]
            right[q] = chunk[:, 512:]

    def tokens(q):
        return jnp.concatenate([left[q, 0:80, :], right[q, 0:80, :]], axis=1)

    def cotangent(q):
        return jnp.concatenate([left[q, 80:160, :], right[q, 80:160, :]], axis=1)

    partner = at(flip=True)
    part_copy = {q: send(r.part_send.at[q], r.part_recv.at[q], partner) for q in range(4)}
    grads = r.grads
    grad_copy = {q: send(grads.at[q], grads.at[q], partner) for q in range(4)}
    xy_copy = {
        q: [
            send(r.xy_send.at[q, lax.rem(x + d, 4)], r.xy_recv.at[q, d], at(dx=d, dy=OFFSET[q]))
            for d in range(4)
            if q or d
        ]
        for q in range(4)
    }

    def products(q):
        for n in range(2):
            yield n * 4, dot_t(tokens(q), w_hidden[n * 512 : n * 512 + 512, :])
        yield 8, dot_t(cotangent(q), w_down[...])

    def give(q):
        for block, value in products(q):
            r.part_send[q, :, block * 128 : block * 128 + 512] = value.astype(BF16)
        part_copy[q].start()

    def keep(q):
        s = OWNER[q][1]
        for block, value in products(q):
            for b in range(4):
                r.part[s, b * 3 + block // 4] = value[:, b * 128 : b * 128 + 128]

    def groups(q):
        return ((0, 2), (2, 1)) if q in (0, 2) else ((2, 1), (0, 2))

    def ring(q):
        s = OWNER[q][1]
        (a0, an), (b0, bn) = groups(q)

        def at_j(ref, d, lo, n):
            return ref.at[s, pl.ds(lax.rem(zh + d, 4) * 3 + lo, n)]

        half = lambda ref, lo, n: ref.at[s, pl.ds(lo, n)]
        mine = r.part_b
        return SimpleNamespace(
            far_a=send(at_j(mine, 2, a0, an), half(r.relay_recv, a0, an), at(dh=1)),
            near_b=send(at_j(mine, 1, b0, bn), half(r.near_recv, b0, bn), at(dh=1)),
            far_b=send(at_j(mine, 2, b0, bn), half(r.relay_recv, b0, bn), at(dh=3)),
            near_a=send(at_j(mine, 3, a0, an), half(r.near_recv, a0, an), at(dh=3)),
            on_a=send(half(r.relay_send, a0, an), half(r.far_recv, a0, an), at(dh=1)),
            on_b=send(half(r.relay_send, b0, bn), half(r.far_recv, b0, bn), at(dh=3)),
        )

    rings = {q: ring(q) for q in range(4)}

    def reduce_start(q):
        s = OWNER[q][1]
        part_copy[q].wait_recv()
        for b in range(4):
            for c in range(3):
                lanes = c * 512 + b * 128
                total = r.part[s, b * 3 + c] + r.part_recv[q, :, lanes : lanes + 128].astype(F32)
                r.part[s, b * 3 + c] = total
                r.part_b[s, b * 3 + c] = total.astype(BF16)
        for copy in (rings[q].far_a, rings[q].far_b, rings[q].near_b, rings[q].near_a):
            copy.start()

    def reduce_relay(q):
        s = OWNER[q][1]
        for (lo, n), d, far, on in (
            (groups(q)[0], 1, rings[q].far_a, rings[q].on_a),
            (groups(q)[1], 3, rings[q].far_b, rings[q].on_b),
        ):
            far.wait_recv()
            base = lax.rem(zh + d, 4) * 3
            for c in range(lo, lo + n):
                total = r.part[s, base + c] + r.relay_recv[s, c].astype(F32)
                r.relay_send[s, c] = total.astype(BF16)
            on.start()

    def gather(q):
        here, low, high = zh, lax.rem(zh + 3, 4), lax.rem(zh + 1, 4)
        return SimpleNamespace(
            up=send(grads.at[q, here], grads.at[q, here], at(dh=1)),
            down=send(grads.at[q, here], grads.at[q, here], at(dh=3)),
            on_up=send(grads.at[q, low, pl.ds(0, 1)], grads.at[q, low, pl.ds(0, 1)], at(dh=1)),
            on_down=send(grads.at[q, high, pl.ds(1, 1)], grads.at[q, high, pl.ds(1, 1)], at(dh=3)),
        )

    gathers = {q: gather(q) for q in range(4)}

    def activate(q):
        s = OWNER[q][1]
        for copy in (rings[q].near_a, rings[q].near_b, rings[q].on_a, rings[q].on_b):
            copy.wait_recv()
        gate, up, hidden_grad = (
            r.part[s, zh * 3 + c] + r.near_recv[s, c].astype(F32) + r.far_recv[s, c].astype(F32) for c in range(3)
        )
        sig = jax.nn.sigmoid(gate)
        grads[q, zh, 0] = (hidden_grad * up * sig * (1.0 + gate * (1.0 - sig))).astype(BF16)
        grads[q, zh, 1] = (hidden_grad * gate * sig).astype(BF16)
        gathers[q].up.start()
        gathers[q].down.start()
        r.hid[s] = (gate * sig * up).astype(BF16)

    def gather_relay(q):
        gathers[q].up.wait_recv()
        gathers[q].on_up.start()
        gathers[q].down.wait_recv()
        gathers[q].on_down.start()

    def gather_end(q):
        gathers[q].on_up.wait_recv()
        gathers[q].on_down.wait_recv()
        grad_copy[q].start()

    def both(q):
        return jnp.concatenate([grads[q, j, c] for c in range(2) for j in range(4)], axis=1)

    def backward(q):
        both_grads = both(q)

        def source(i, j):
            part = jnp.where(i >= 24, 1, 0) + jnp.where(i >= 48, 1, 0) + jnp.where(i >= 72, 1, 0)
            inside = i - 24 * part
            return (inside < 20) & (j == part * 20 + inside)

        spread = one_hot(96, 80, source)
        for n in range(2):
            value = dot(both_grads, w_hidden[:, n * 512 : n * 512 + 512]).astype(BF16)
            wide = dot(spread, value).astype(BF16)
            for m in range(4):
                r.xy_send[q, m, :, n * 512 : n * 512 + 512] = wide[24 * m : 24 * m + 24]
        for copy in xy_copy[q]:
            copy.start()

    def take(q):
        grad_copy[q].wait_recv()
        backward(q)

    lt_core = send(r.lt_b.at[1 - k], r.lt_crecv, partner)
    lt_shard = lambda d, half: r.lt_two_b.at[lax.rem(zh + d, 4), half]
    lt_first = [send(lt_shard(2, half), r.lt_relay_recv.at[half], at(dh=(1, 3)[half])) for half in range(2)]
    lt_first += [send(lt_shard((3, 1)[half], half), r.lt_near.at[half], at(dh=(3, 1)[half])) for half in range(2)]
    lt_second = [send(r.lt_relay_send.at[half], r.lt_far.at[half], at(dh=(1, 3)[half])) for half in range(2)]
    lt_y = [send(r.lt.at[0], r.lt.at[q], at(dy=(4 - OFFSET[q]) % 4)) for q in (1, 2, 3)]

    def low_start():
        for b in range(2):
            low = dot(tokens(0), r.new_in[b])
            low = jnp.concatenate([low, jnp.zeros((48, 128), F32)], axis=0).T
            for c in range(8):
                value = low[16 * c : 16 * c + 16, :]
                r.lt_f[c % 2, c // 2, 16 * b : 16 * b + 16, :] = value
                r.lt_b[c % 2, c // 2, 16 * b : 16 * b + 16, :] = value.astype(BF16)
        lt_core.start()

    def low_middle():
        lt_core.wait_recv()
        for j in range(4):
            for half in range(2):
                rows = slice(16 * half, 16 * half + 16)
                total = r.lt_f[k, j, rows, :] + r.lt_crecv[j, rows, :].astype(F32)
                r.lt_two[j, half] = total
                r.lt_two_b[j, half] = total.astype(BF16)
        for copy in lt_first:
            copy.start()

    def low_relay():
        for half in range(2):
            lt_first[half].wait_recv()
            total = r.lt_two[lax.rem(zh + (1, 3)[half], 4), half] + r.lt_relay_recv[half].astype(F32)
            r.lt_relay_send[half] = total.astype(BF16)
            lt_second[half].start()

    def low_end():
        for half in range(2):
            lt_first[2 + half].wait_recv()
            lt_second[half].wait_recv()
            total = r.lt_two[zh, half] + r.lt_near[half].astype(F32) + r.lt_far[half].astype(F32)
            r.lt[0, 16 * half : 16 * half + 16, :] = total.astype(BF16)
        for copy in lt_y:
            copy.start()

    d_x = [send(r.d_part.at[lax.rem(x + d, 4)], r.d_xrecv.at[d], at(dx=d)) for d in (1, 2, 3)]
    d_z = [send(r.d_sum.at[lax.rem(zl + d, 4)], r.d_zrecv.at[d], at(dz=d)) for d in (1, 2, 3)]
    d_h = [send(r.d_col, r.d_crecv.at[d], at(dh=d)) for d in (1, 3)]
    d_h += [send(r.d_crecv.at[1], r.d_crecv.at[2], at(dh=1))]
    d_k = send(r.d_both.at[0, k], r.d_both.at[0, k], partner)
    d_y = [send(r.d_both.at[0], r.d_both.at[d], at(dy=4 - d)) for d in (1, 2, 3)]

    def down_x():
        for s in range(2):
            value = dot_t(r.new_down_t[zh], r.hid[s])
            value = jnp.concatenate([value, jnp.zeros((128, 48), F32)], axis=1)
            for n in range(4):
                r.d_part[n, :, s * 128 : s * 128 + 128] = value[32 * n : 32 * n + 32]
        for copy in d_x:
            copy.start()

    def down_z():
        total = r.d_part[x]
        for d, copy in zip((1, 2, 3), d_x):
            copy.wait_recv()
            total += r.d_xrecv[d]
        for n in range(4):
            r.d_sum[n] = total[8 * n : 8 * n + 8]
        for copy in d_z:
            copy.start()

    def down_h():
        total = r.d_sum[zl]
        for d, copy in zip((1, 2, 3), d_z):
            copy.wait_recv()
            total += r.d_zrecv[d]
        r.d_col[...] = total
        d_h[0].start()
        d_h[1].start()

    def down_relay():
        d_h[0].wait_recv()
        d_h[2].start()

    def down_k():
        d_h[1].wait_recv()
        d_h[2].wait_recv()
        total = r.d_col[...] + r.d_crecv[1] + r.d_crecv[2] + r.d_crecv[3]
        r.d_both[0, k] = total
        d_k.start()

    def down_y():
        d_k.wait_recv()
        for copy in d_y:
            copy.start()

    def down_end():
        for copy in d_y:
            copy.wait_recv()
        out = None
        for q in range(4):
            total = None
            for d in range(4):
                core, s = OWNER[SLOT[(OFFSET[q] - d) % 4]]
                term = r.d_both[d, core, :, s * 128 : s * 128 + 128]
                total = term if total is None else total + term
            term = dot(total[:, 0:80].astype(BF16), cotangent(q))
            out = term if out is None else out + term
        mine = out[0:2]
        for n in (1, 2, 3):
            mine = jnp.where(y == n, out[2 * n : 2 * n + 2], mine)
        gd_out[...] = SCALE * mine

    orders = (
        (
            (keep, 0), (reduce_start, 0), (low_start,), (low_middle,), (build, 1), (give, 1), (reduce_relay, 0),
            (build, 2), (give, 2), (build, 3), (keep, 3), (reduce_start, 3), (low_relay,), (activate, 0),
            (reduce_relay, 3), (gather_relay, 0), (low_end,), (gather_end, 0), (backward, 0), (activate, 3), (down_x,),
            (take, 1), (gather_relay, 3), (down_z,), (take, 2), (gather_end, 3), (backward, 3),
        ),
        (
            (give, 0), (low_start,), (low_middle,), (build, 1), (keep, 1), (reduce_start, 1), (build, 2), (keep, 2),
            (reduce_start, 2), (build, 3), (give, 3), (low_relay,), (reduce_relay, 1), (reduce_relay, 2),
            (activate, 1), (activate, 2), (down_x,), (low_end,), (gather_relay, 1), (gather_relay, 2), (take, 0),
            (gather_end, 1), (backward, 1), (gather_end, 2), (backward, 2), (down_z,), (take, 3),
        ),
    )
    for core in range(2):

        @pl.when(k == core)
        def _():
            for step, *args in orders[core]:
                step(*args)

    def flush(copies):
        for copy in copies:
            copy.wait_send()

    down_h()
    flush(first + second + over_y + [to_up, to_down, lt_core] + over_x[1] + over_x[2] + over_x[3])
    flush(lt_first + lt_second)
    for copy in lt_y:
        copy.wait_recv()
    for b in range(2):
        out = None
        for q in range(4):
            columns = jnp.concatenate([grads[q, j, b] for j in range(4)], axis=1)
            term = dot(r.lt[q, 16 * b : 16 * b + 16, 0:80], columns)
            out = term if out is None else out + term
        gh_out[b] = SCALE * out[:, 0:448]
    for core in range(2):

        @pl.when(k == core)
        def _():
            for q in OWNED[core]:
                flush(list(vars(rings[q]).values()) + list(vars(gathers[q]).values()) + [grad_copy[q]])
            flush([part_copy[q] for q in OWNED[1 - core]])

    flush(d_x + d_z + lt_y)
    down_relay()
    total = r.xy_send[0, x].astype(F32)
    for q in (0, 1, 2, 3):
        if q == 3:
            down_k()
            down_y()
        for copy in xy_copy[q]:
            copy.wait_recv()
        for d in range(4):
            if q or d:
                total += r.xy_recv[q, d].astype(F32)
    spread = one_hot(32, 24, lambda i, j: ((i & 7) < 5) & (j == (i >> 3) * 5 + (i & 7)))
    wide = dot(spread, total.astype(BF16))
    for n in range(4):
        r.z_own[n] = wide[8 * n : 8 * n + 8]
        r.z_send[n] = wide[8 * n : 8 * n + 8].astype(BF16)
    z_copies = [send(r.z_send.at[lax.rem(zl + d, 4)], r.z_recv.at[d], at(dz=d)) for d in (1, 2, 3)]
    for copy in z_copies:
        copy.start()
    flush(d_h + [d_k] + d_y + xy_copy[0] + xy_copy[1] + xy_copy[2] + xy_copy[3])
    down_end()
    total = r.z_own[zl]
    for d, copy in zip((1, 2, 3), z_copies):
        copy.wait_recv()
        total += r.z_recv[d].astype(F32)
    ig_out[...] = total.astype(BF16)
    flush(z_copies)


def moments(*refs):
    ins, outs, ins_v, outs_v = refs[:9], refs[9:14], refs[14:23], refs[23:28]
    in_sem, out_sem = refs[28:]
    loads = [pltpu.make_async_copy(a, b, in_sem.at[n]) for n, (a, b) in enumerate(zip(ins, ins_v))]
    stores = [pltpu.make_async_copy(a, b, out_sem.at[n]) for n, (a, b) in enumerate(zip(outs_v, outs))]
    for copy in loads:
        copy.start()
    for copy in loads:
        copy.wait()
    ig, grad_hidden, grad_down, first_hidden, second_hidden, first_down, second_down, keep_hidden, keep_down = ins_v
    outs_v[0][...] = ig[0:5, :]
    stores[0].start()
    keep = keep_hidden[...].astype(F32)
    for n in range(2):
        kept = jnp.broadcast_to(keep[n : n + 1, :], (16, 448))
        grad = grad_hidden[n]
        outs_v[1][n] = 0.9 * kept * first_hidden[n] + 0.1 * grad
        outs_v[2][n] = 0.999 * kept * second_hidden[n] + 0.001 * grad * grad
    stores[1].start()
    stores[2].start()
    kept = jnp.broadcast_to(keep_down[...].astype(F32), (2, 1024))
    grad = grad_down[...]
    outs_v[3][...] = 0.9 * kept * first_down[...] + 0.1 * grad
    outs_v[4][...] = 0.999 * kept * second_down[...] + 0.001 * grad * grad
    stores[3].start()
    stores[4].start()
    for copy in stores:
        copy.wait()


def body(
    tokens, cotangent, gate_weight, up_weight, down_weight, old_in_hidden, old_out_hidden, old_in_down,
    old_out_down, new_in_hidden, new_in_down, first_hidden, second_hidden, first_down, second_down,
    keep_hidden, keep_down,
):
    vmem = pl.BlockSpec(memory_space=pltpu.VMEM)
    far = pl.BlockSpec(memory_space=pltpu.HBM)
    ig, grad_hidden, grad_down = pl.pallas_call(
        kernel,
        out_shape=(
            jax.ShapeDtypeStruct((8, 1024), BF16),
            jax.ShapeDtypeStruct((2, 16, 448), F32),
            jax.ShapeDtypeStruct((2, 1024), F32),
        ),
        in_specs=[far] * len(INPUTS),
        out_specs=(vmem, vmem, vmem),
        scratch_shapes=[pltpu.VMEM(shape, BF16) for shape in INPUTS.values()]
        + [pltpu.VMEM(*spec) for spec in SCRATCH.values()]
        + [pltpu.SemaphoreType.DMA((N_SEM,)), pltpu.SemaphoreType.DMA((N_SEM,)), pltpu.SemaphoreType.DMA((len(INPUTS),))],
        compiler_params=pltpu.CompilerParams(
            collective_id=0, has_side_effects=True, vmem_limit_bytes=63 * 2**20
        ),
        cost_estimate=pl.CostEstimate(flops=2_000_000_000, bytes_accessed=4_000_000, transcendentals=150_000),
        name="layer",
    )(
        tokens, cotangent, gate_weight.T, up_weight.T, down_weight, old_in_hidden, old_out_hidden.transpose(0, 2, 1),
        old_in_down, old_out_down, new_in_hidden, new_in_down,
    )
    sources = (
        ig, grad_hidden, grad_down, first_hidden, second_hidden, first_down, second_down, keep_hidden,
        keep_down.reshape(1, 1024),
    )
    results = (
        jax.ShapeDtypeStruct((5, 1024), BF16),
        jax.ShapeDtypeStruct((2, 16, 448), F32),
        jax.ShapeDtypeStruct((2, 16, 448), F32),
        jax.ShapeDtypeStruct((2, 1024), F32),
        jax.ShapeDtypeStruct((2, 1024), F32),
    )
    return pl.pallas_call(
        moments,
        out_shape=results,
        in_specs=[far] * len(sources),
        out_specs=[far] * len(results),
        scratch_shapes=[pltpu.VMEM(a.shape, a.dtype) for a in sources + results]
        + [pltpu.SemaphoreType.DMA((len(sources),)), pltpu.SemaphoreType.DMA((len(results),))],
        compiler_params=pltpu.CompilerParams(vmem_limit_bytes=63 * 2**20),
        name="moments",
    )(*sources)


def solution(mesh):
    return jax.shard_map(
        body,
        mesh=mesh,
        in_specs=(
            P("row", "col"), P("row", "col"), P("col", "row"), P("col", "row"), P("row", "col"),
            P(None, "col", None), P(None, None, "row"), P("row", None), P(None, "col"), P(None, "col", None),
            P("row", None), P(None, "col", "row"), P(None, "col", "row"), P("row", "col"), P("row", "col"),
            P(None, "row"), P("col"),
        ),
        out_specs=(
            P("row", "col"), P(None, "col", "row"), P(None, "col", "row"), P("row", "col"), P("row", "col"),
        ),
        check_vma=False,
    )
```

```python
from types import SimpleNamespace

import jax
import jax.numpy as jnp
from jax import lax
from jax.experimental import pallas as pl
from jax.experimental.pallas import tpu as pltpu
from jax.sharding import PartitionSpec as P

MESH = pl.DeviceIdType.MESH
F32 = jnp.float32
BF16 = jnp.bfloat16
SCALE = 0.25
OWNED = ((0, 3), (1, 2))
OFFSET = (0, 1, 3, 2)
SLOT = {o: q for q, o in enumerate(OFFSET)}
OWNER = {q: (k, s) for k, qs in enumerate(OWNED) for s, q in enumerate(qs)}


def dot(a, b):
    return lax.dot_general(a, b, (((1,), (0,)), ((), ())), preferred_element_type=F32)


def dot_t(a, b):
    return lax.dot_general(a, b, (((1,), (1,)), ((), ())), preferred_element_type=F32)


def one_hot(rows, cols, source):
    i = lax.broadcasted_iota(jnp.int32, (rows, cols), 0)
    j = lax.broadcasted_iota(jnp.int32, (rows, cols), 1)
    return jnp.where(source(i, j), 1.0, 0.0).astype(BF16)


SCRATCH = dict(
    w_hidden=((1024, 1024), BF16),
    w_down=((512, 1024), BF16),
    new_down_t=((4, 128, 128), BF16),
    units=((4, 16, 1024), BF16),
    quads=((4, 40, 1024), BF16),
    strip=((40, 512), BF16),
    strips=((2, 4, 40, 512), BF16),
    far_quads=((4, 40, 1024), BF16),
    left=((4, 160, 512), BF16),
    right=((4, 160, 512), BF16),
    part_send=((4, 80, 1536), BF16),
    part_recv=((4, 80, 1536), BF16),
    part=((2, 12, 80, 128), F32),
    part_b=((2, 12, 80, 128), BF16),
    relay_recv=((2, 3, 80, 128), BF16),
    relay_send=((2, 3, 80, 128), BF16),
    near_recv=((2, 3, 80, 128), BF16),
    far_recv=((2, 3, 80, 128), BF16),
    grads=((4, 4, 2, 80, 128), BF16),
    hid=((2, 80, 128), BF16),
    xy_send=((4, 4, 24, 1024), BF16),
    xy_recv=((4, 4, 24, 1024), BF16),
    z_own=((4, 8, 1024), F32),
    z_send=((4, 8, 1024), BF16),
    z_recv=((4, 8, 1024), BF16),
    d_part=((4, 32, 256), F32),
    d_xrecv=((4, 32, 256), F32),
    d_sum=((4, 8, 256), F32),
    d_zrecv=((4, 8, 256), F32),
    d_col=((8, 256), F32),
    d_crecv=((4, 8, 256), F32),
    d_both=((4, 2, 8, 256), F32),
    lt_f=((2, 4, 32, 128), F32),
    lt_b=((2, 4, 32, 128), BF16),
    lt_crecv=((4, 32, 128), BF16),
    lt_two=((4, 2, 16, 128), F32),
    lt_two_b=((4, 2, 16, 128), BF16),
    lt_relay_recv=((2, 16, 128), BF16),
    lt_relay_send=((2, 16, 128), BF16),
    lt_near=((2, 16, 128), BF16),
    lt_far=((2, 16, 128), BF16),
    lt=((4, 32, 128), BF16),
)
INPUTS = dict(
    tokens=(5, 1024), cotangent=(5, 1024), gate_raw=(448, 1024), up_raw=(448, 1024), down_raw=(448, 1024),
    in_raw=(2, 1024, 128), out_hidden=(2, 448, 128), in_down=(448, 128), out_down=(128, 1024),
    new_in=(2, 1024, 128), new_down=(448, 128),
)
N_SEM = 112


def kernel(*refs):
    n_in = len(INPUTS)
    ig_out, gh_out, gd_out = refs[n_in : n_in + 3]
    far = SimpleNamespace(**dict(zip(INPUTS, refs[:n_in])))
    inner = refs[n_in + 3 :]
    r = SimpleNamespace(**dict(zip(list(INPUTS) + list(SCRATCH), inner)))
    send_sem, recv_sem, local_sem = inner[n_in + len(SCRATCH) :]

    row, col = lax.axis_index("row"), lax.axis_index("col")
    x, zl, y = row // 16, lax.rem(row // 4, 4), lax.rem(row, 4)
    zh, k = col // 2, lax.rem(col, 2)

    def at(dx=0, dz=0, dy=0, dh=0, flip=False):
        to_row = lax.rem(x + dx, 4) * 16 + lax.rem(zl + dz, 4) * 4 + lax.rem(y + dy, 4)
        return (to_row, lax.rem(zh + dh, 4) * 2 + (1 - k if flip else k))

    peers = [at(dx=d) for d in (1, 2, 3)] + [at(dz=d) for d in (1, 2, 3)]
    peers += [at(dx=d, dy=e) for d in range(4) for e in (1, 2, 3)] + [at(dh=d) for d in (1, 3)] + [at(flip=True)]
    barrier = pltpu.get_barrier_semaphore()
    for peer in peers:
        pl.semaphore_signal(barrier, inc=1, device_id=peer, device_id_type=MESH)

    loads = SimpleNamespace()
    for n, (name, ref) in enumerate(vars(far).items()):
        copy = pltpu.make_async_copy(ref, vars(r)[name], local_sem.at[n])
        copy.start()
        vars(loads)[name] = copy

    ids = []

    def send(src, dst, to):
        n = len(ids)
        ids.append(n)
        return pltpu.make_async_remote_copy(
            src_ref=src, dst_ref=dst, send_sem=send_sem.at[n], recv_sem=recv_sem.at[n], device_id=to, device_id_type=MESH
        )

    units = r.units
    units[zl] = jnp.zeros((16, 1024), BF16)
    loads.tokens.wait()
    loads.cotangent.wait()
    units[zl, pl.ds(0, 5), :] = r.tokens[...]
    units[zl, pl.ds(8, 5), :] = r.cotangent[...]
    pl.semaphore_wait(barrier, len(peers))
    first = [send(units.at[zl], units.at[zl], at(dz=d)) for d in (1, 2, 3)]
    for copy in first:
        copy.start()

    for copy in list(vars(loads).values())[2:]:
        copy.wait()
    w_hidden, w_down = r.w_hidden, r.w_down

    def merge_rows(n, _):
        rows = pl.ds(pl.multiple_of(n * 224, 224), 224)
        for b, raw in enumerate((r.gate_raw, r.up_raw)):
            step = dot_t(r.out_hidden[b, rows, :], r.in_raw[b])
            to = pl.ds(pl.multiple_of(b * 512 + n * 224, 32), 224)
            w_hidden[to, :] = (raw[rows, :].astype(F32) + SCALE * step).astype(BF16)
        step = dot(r.in_down[rows, :], r.out_down[...])
        w_down[rows, :] = (r.down_raw[rows, :].astype(F32) + SCALE * step).astype(BF16)
        return 0

    lax.fori_loop(0, 2, merge_rows, 0)
    for n in range(2):
        w_hidden[n * 512 + 448 : n * 512 + 512, :] = jnp.zeros((64, 1024), BF16)
    w_down[448:512, :] = jnp.zeros((64, 1024), BF16)
    for j in range(3):
        r.new_down_t[j] = r.new_down[128 * j : 128 * j + 128, :].astype(F32).T.astype(BF16)
    last = jnp.concatenate([r.new_down[384:448, :].astype(F32), jnp.zeros((64, 128), F32)], axis=0)
    r.new_down_t[3] = last.T.astype(BF16)

    for copy in first:
        copy.wait_recv()
    pick = one_hot(40, 64, lambda i, j: ((j & 7) < 5) & (i == ((j >> 3) & 1) * 20 + (j >> 4) * 5 + (j & 7)))
    quads, strip, strips, far_quads = r.quads, r.strip, r.strips, r.far_quads
    left, right = r.left, r.right
    quad = dot(pick, units[...].reshape(64, 1024)).astype(BF16)
    quads[x] = quad
    strip[...] = quad[:, 512:]
    second = [send(quads.at[x], quads.at[x], at(dx=d)) for d in (1, 2, 3)]
    over_y = [send(strip, strips.at[0, x], at(dy=3)), send(strip, strips.at[1, x], at(dy=1))]
    over_y += [send(quads.at[x], far_quads.at[x], at(dy=2))]
    for copy in second + over_y:
        copy.start()

    def arrange(get):
        total = None
        for n in range(4):
            place = one_hot(160, 40, lambda i, j, n=n: i == n * 20 + j + jnp.where(j >= 20, 60, 0))
            term = dot(place, get(n))
            total = term if total is None else total + term
        return total.astype(BF16)

    for copy in second:
        copy.wait_recv()
    chunk = arrange(lambda n: quads[n])
    left[0] = chunk[:, :512]
    right[0] = chunk[:, 512:]

    to_up = send(left.at[0], left.at[2], at(dy=1))
    to_down = send(left.at[0], left.at[1], at(dy=3))
    over_x = {
        q: [send(ref.at[x], ref.at[x], at(dx=d)) for d in (1, 2, 3)]
        for q, ref in ((1, strips.at[0]), (2, strips.at[1]), (3, far_quads))
    }
    to_up.start()
    to_down.start()
    for q in (1, 2, 3):
        over_y[q - 1].wait_recv()
        for copy in over_x[q]:
            copy.start()

    def build(q):
        if q < 3:
            (to_down, to_up)[q - 1].wait_recv()
        for copy in over_x[q]:
            copy.wait_recv()
        if q < 3:
            right[q] = arrange(lambda n: strips[q - 1, n])
        else:
            chunk = arrange(lambda n: far_quads[n])
            left[q] = chunk[:, :512]
            right[q] = chunk[:, 512:]

    def tokens(q):
        return jnp.concatenate([left[q, 0:80, :], right[q, 0:80, :]], axis=1)

    def cotangent(q):
        return jnp.concatenate([left[q, 80:160, :], right[q, 80:160, :]], axis=1)

    partner = at(flip=True)
    part_copy = {q: send(r.part_send.at[q], r.part_recv.at[q], partner) for q in range(4)}
    grads = r.grads
    grad_copy = {q: send(grads.at[q], grads.at[q], partner) for q in range(4)}
    xy_copy = {
        q: [
            send(r.xy_send.at[q, lax.rem(x + d, 4)], r.xy_recv.at[q, d], at(dx=d, dy=OFFSET[q]))
            for d in range(4)
            if q or d
        ]
        for q in range(4)
    }

    def products(q):
        for n in range(2):
            yield n * 4, dot_t(tokens(q), w_hidden[n * 512 : n * 512 + 512, :])
        yield 8, dot_t(cotangent(q), w_down[...])

    def give(q):
        for block, value in products(q):
            r.part_send[q, :, block * 128 : block * 128 + 512] = value.astype(BF16)
        part_copy[q].start()

    def keep(q):
        s = OWNER[q][1]
        for block, value in products(q):
            for b in range(4):
                r.part[s, b * 3 + block // 4] = value[:, b * 128 : b * 128 + 128]

    def groups(q):
        return ((0, 2), (2, 1)) if q in (0, 2) else ((2, 1), (0, 2))

    def ring(q):
        s = OWNER[q][1]
        (a0, an), (b0, bn) = groups(q)

        def at_j(ref, d, lo, n):
            return ref.at[s, pl.ds(lax.rem(zh + d, 4) * 3 + lo, n)]

        half = lambda ref, lo, n: ref.at[s, pl.ds(lo, n)]
        mine = r.part_b
        return SimpleNamespace(
            far_a=send(at_j(mine, 2, a0, an), half(r.relay_recv, a0, an), at(dh=1)),
            near_b=send(at_j(mine, 1, b0, bn), half(r.near_recv, b0, bn), at(dh=1)),
            far_b=send(at_j(mine, 2, b0, bn), half(r.relay_recv, b0, bn), at(dh=3)),
            near_a=send(at_j(mine, 3, a0, an), half(r.near_recv, a0, an), at(dh=3)),
            on_a=send(half(r.relay_send, a0, an), half(r.far_recv, a0, an), at(dh=1)),
            on_b=send(half(r.relay_send, b0, bn), half(r.far_recv, b0, bn), at(dh=3)),
        )

    rings = {q: ring(q) for q in range(4)}

    def reduce_start(q):
        s = OWNER[q][1]
        part_copy[q].wait_recv()
        for b in range(4):
            for c in range(3):
                lanes = c * 512 + b * 128
                total = r.part[s, b * 3 + c] + r.part_recv[q, :, lanes : lanes + 128].astype(F32)
                r.part[s, b * 3 + c] = total
                r.part_b[s, b * 3 + c] = total.astype(BF16)
        for copy in (rings[q].far_a, rings[q].far_b, rings[q].near_b, rings[q].near_a):
            copy.start()

    def reduce_relay(q):
        s = OWNER[q][1]
        for (lo, n), d, far, on in (
            (groups(q)[0], 1, rings[q].far_a, rings[q].on_a),
            (groups(q)[1], 3, rings[q].far_b, rings[q].on_b),
        ):
            far.wait_recv()
            base = lax.rem(zh + d, 4) * 3
            for c in range(lo, lo + n):
                total = r.part[s, base + c] + r.relay_recv[s, c].astype(F32)
                r.relay_send[s, c] = total.astype(BF16)
            on.start()

    def gather(q):
        here, low, high = zh, lax.rem(zh + 3, 4), lax.rem(zh + 1, 4)
        return SimpleNamespace(
            up=send(grads.at[q, here], grads.at[q, here], at(dh=1)),
            down=send(grads.at[q, here], grads.at[q, here], at(dh=3)),
            on_up=send(grads.at[q, low, pl.ds(0, 1)], grads.at[q, low, pl.ds(0, 1)], at(dh=1)),
            on_down=send(grads.at[q, high, pl.ds(1, 1)], grads.at[q, high, pl.ds(1, 1)], at(dh=3)),
        )

    gathers = {q: gather(q) for q in range(4)}

    def activate(q):
        s = OWNER[q][1]
        for copy in (rings[q].near_a, rings[q].near_b, rings[q].on_a, rings[q].on_b):
            copy.wait_recv()
        gate, up, hidden_grad = (
            r.part[s, zh * 3 + c] + r.near_recv[s, c].astype(F32) + r.far_recv[s, c].astype(F32) for c in range(3)
        )
        sig = jax.nn.sigmoid(gate)
        grads[q, zh, 0] = (hidden_grad * up * sig * (1.0 + gate * (1.0 - sig))).astype(BF16)
        grads[q, zh, 1] = (hidden_grad * gate * sig).astype(BF16)
        gathers[q].up.start()
        gathers[q].down.start()
        r.hid[s] = (gate * sig * up).astype(BF16)

    def gather_relay(q):
        gathers[q].up.wait_recv()
        gathers[q].on_up.start()
        gathers[q].down.wait_recv()
        gathers[q].on_down.start()

    def gather_end(q):
        gathers[q].on_up.wait_recv()
        gathers[q].on_down.wait_recv()
        grad_copy[q].start()

    def both(q):
        return jnp.concatenate([grads[q, j, c] for c in range(2) for j in range(4)], axis=1)

    def backward(q):
        both_grads = both(q)

        def source(i, j):
            part = jnp.where(i >= 24, 1, 0) + jnp.where(i >= 48, 1, 0) + jnp.where(i >= 72, 1, 0)
            inside = i - 24 * part
            return (inside < 20) & (j == part * 20 + inside)

        spread = one_hot(96, 80, source)
        for n in range(2):
            value = dot(both_grads, w_hidden[:, n * 512 : n * 512 + 512]).astype(BF16)
            wide = dot(spread, value).astype(BF16)
            for m in range(4):
                r.xy_send[q, m, :, n * 512 : n * 512 + 512] = wide[24 * m : 24 * m + 24]
        for copy in xy_copy[q]:
            copy.start()

    def take(q):
        grad_copy[q].wait_recv()
        backward(q)

    lt_core = send(r.lt_b.at[1 - k], r.lt_crecv, partner)
    lt_shard = lambda d, half: r.lt_two_b.at[lax.rem(zh + d, 4), half]
    lt_first = [send(lt_shard(2, half), r.lt_relay_recv.at[half], at(dh=(1, 3)[half])) for half in range(2)]
    lt_first += [send(lt_shard((3, 1)[half], half), r.lt_near.at[half], at(dh=(3, 1)[half])) for half in range(2)]
    lt_second = [send(r.lt_relay_send.at[half], r.lt_far.at[half], at(dh=(1, 3)[half])) for half in range(2)]
    lt_y = [send(r.lt.at[0], r.lt.at[q], at(dy=(4 - OFFSET[q]) % 4)) for q in (1, 2, 3)]

    def low_start():
        for b in range(2):
            low = dot(tokens(0), r.new_in[b])
            low = jnp.concatenate([low, jnp.zeros((48, 128), F32)], axis=0).T
            for c in range(8):
                value = low[16 * c : 16 * c + 16, :]
                r.lt_f[c % 2, c // 2, 16 * b : 16 * b + 16, :] = value
                r.lt_b[c % 2, c // 2, 16 * b : 16 * b + 16, :] = value.astype(BF16)
        lt_core.start()

    def low_middle():
        lt_core.wait_recv()
        for j in range(4):
            for half in range(2):
                rows = slice(16 * half, 16 * half + 16)
                total = r.lt_f[k, j, rows, :] + r.lt_crecv[j, rows, :].astype(F32)
                r.lt_two[j, half] = total
                r.lt_two_b[j, half] = total.astype(BF16)
        for copy in lt_first:
            copy.start()

    def low_relay():
        for half in range(2):
            lt_first[half].wait_recv()
            total = r.lt_two[lax.rem(zh + (1, 3)[half], 4), half] + r.lt_relay_recv[half].astype(F32)
            r.lt_relay_send[half] = total.astype(BF16)
            lt_second[half].start()

    def low_end():
        for half in range(2):
            lt_first[2 + half].wait_recv()
            lt_second[half].wait_recv()
            total = r.lt_two[zh, half] + r.lt_near[half].astype(F32) + r.lt_far[half].astype(F32)
            r.lt[0, 16 * half : 16 * half + 16, :] = total.astype(BF16)
        for copy in lt_y:
            copy.start()

    d_x = [send(r.d_part.at[lax.rem(x + d, 4)], r.d_xrecv.at[d], at(dx=d)) for d in (1, 2, 3)]
    d_z = [send(r.d_sum.at[lax.rem(zl + d, 4)], r.d_zrecv.at[d], at(dz=d)) for d in (1, 2, 3)]
    d_h = [send(r.d_col, r.d_crecv.at[d], at(dh=d)) for d in (1, 3)]
    d_h += [send(r.d_crecv.at[1], r.d_crecv.at[2], at(dh=1))]
    d_k = send(r.d_both.at[0, k], r.d_both.at[0, k], partner)
    d_y = [send(r.d_both.at[0], r.d_both.at[d], at(dy=4 - d)) for d in (1, 2, 3)]

    def down_x():
        for s in range(2):
            value = dot_t(r.new_down_t[zh], r.hid[s])
            value = jnp.concatenate([value, jnp.zeros((128, 48), F32)], axis=1)
            for n in range(4):
                r.d_part[n, :, s * 128 : s * 128 + 128] = value[32 * n : 32 * n + 32]
        for copy in d_x:
            copy.start()

    def down_z():
        total = r.d_part[x]
        for d, copy in zip((1, 2, 3), d_x):
            copy.wait_recv()
            total += r.d_xrecv[d]
        for n in range(4):
            r.d_sum[n] = total[8 * n : 8 * n + 8]
        for copy in d_z:
            copy.start()

    def down_h():
        total = r.d_sum[zl]
        for d, copy in zip((1, 2, 3), d_z):
            copy.wait_recv()
            total += r.d_zrecv[d]
        r.d_col[...] = total
        d_h[0].start()
        d_h[1].start()

    def down_relay():
        d_h[0].wait_recv()
        d_h[2].start()

    def down_k():
        d_h[1].wait_recv()
        d_h[2].wait_recv()
        total = r.d_col[...] + r.d_crecv[1] + r.d_crecv[2] + r.d_crecv[3]
        r.d_both[0, k] = total
        d_k.start()

    def down_y():
        d_k.wait_recv()
        for copy in d_y:
            copy.start()

    def down_end():
        for copy in d_y:
            copy.wait_recv()
        out = None
        for q in range(4):
            total = None
            for d in range(4):
                core, s = OWNER[SLOT[(OFFSET[q] - d) % 4]]
                term = r.d_both[d, core, :, s * 128 : s * 128 + 128]
                total = term if total is None else total + term
            term = dot(total[:, 0:80].astype(BF16), cotangent(q))
            out = term if out is None else out + term
        mine = out[0:2]
        for n in (1, 2, 3):
            mine = jnp.where(y == n, out[2 * n : 2 * n + 2], mine)
        gd_out[...] = SCALE * mine

    orders = (
        (
            (keep, 0), (reduce_start, 0), (low_start,), (low_middle,), (build, 1), (give, 1), (reduce_relay, 0),
            (build, 2), (give, 2), (build, 3), (keep, 3), (reduce_start, 3), (low_relay,), (activate, 0),
            (reduce_relay, 3), (gather_relay, 0), (low_end,), (gather_end, 0), (backward, 0), (activate, 3), (down_x,),
            (gather_relay, 3), (down_z,), (take, 1), (take, 2), (down_h,), (gather_end, 3), (backward, 3),
        ),
        (
            (give, 0), (low_start,), (low_middle,), (build, 1), (keep, 1), (reduce_start, 1), (build, 2), (keep, 2),
            (reduce_start, 2), (build, 3), (give, 3), (low_relay,), (reduce_relay, 1), (reduce_relay, 2),
            (activate, 1), (activate, 2), (down_x,), (low_end,), (gather_relay, 1), (gather_relay, 2), (down_z,), (take, 0),
            (gather_end, 1), (backward, 1), (down_h,), (gather_end, 2), (backward, 2), (take, 3),
        ),
    )
    for core in range(2):

        @pl.when(k == core)
        def _():
            for step, *args in orders[core]:
                step(*args)

    def flush(copies):
        for copy in copies:
            copy.wait_send()

    flush(first + second + over_y + [to_up, to_down, lt_core] + over_x[1] + over_x[2] + over_x[3])
    flush(lt_first + lt_second)
    for copy in lt_y:
        copy.wait_recv()
    for b in range(2):
        out = None
        for q in range(4):
            columns = jnp.concatenate([grads[q, j, b] for j in range(4)], axis=1)
            term = dot(r.lt[q, 16 * b : 16 * b + 16, 0:80], columns)
            out = term if out is None else out + term
        gh_out[b] = SCALE * out[:, 0:448]
    for core in range(2):

        @pl.when(k == core)
        def _():
            for q in OWNED[core]:
                flush(list(vars(rings[q]).values()) + list(vars(gathers[q]).values()) + [grad_copy[q]])
            flush([part_copy[q] for q in OWNED[1 - core]])

    flush(d_x + d_z + lt_y)
    down_relay()
    total = r.xy_send[0, x].astype(F32)
    for q in (0, 1, 2, 3):
        if q == 3:
            down_k()
            down_y()
        for copy in xy_copy[q]:
            copy.wait_recv()
        for d in range(4):
            if q or d:
                total += r.xy_recv[q, d].astype(F32)
    spread = one_hot(32, 24, lambda i, j: ((i & 7) < 5) & (j == (i >> 3) * 5 + (i & 7)))
    wide = dot(spread, total.astype(BF16))
    for n in range(4):
        r.z_own[n] = wide[8 * n : 8 * n + 8]
        r.z_send[n] = wide[8 * n : 8 * n + 8].astype(BF16)
    z_copies = [send(r.z_send.at[lax.rem(zl + d, 4)], r.z_recv.at[d], at(dz=d)) for d in (1, 2, 3)]
    for copy in z_copies:
        copy.start()
    flush(d_h + [d_k] + d_y + xy_copy[0] + xy_copy[1] + xy_copy[2] + xy_copy[3])
    down_end()
    total = r.z_own[zl]
    for d, copy in zip((1, 2, 3), z_copies):
        copy.wait_recv()
        total += r.z_recv[d].astype(F32)
    ig_out[...] = total.astype(BF16)
    flush(z_copies)


def moments(*refs):
    ins, outs, ins_v, outs_v = refs[:9], refs[9:14], refs[14:23], refs[23:28]
    in_sem, out_sem = refs[28:]
    loads = [pltpu.make_async_copy(a, b, in_sem.at[n]) for n, (a, b) in enumerate(zip(ins, ins_v))]
    stores = [pltpu.make_async_copy(a, b, out_sem.at[n]) for n, (a, b) in enumerate(zip(outs_v, outs))]
    for copy in loads:
        copy.start()
    for copy in loads:
        copy.wait()
    ig, grad_hidden, grad_down, first_hidden, second_hidden, first_down, second_down, keep_hidden, keep_down = ins_v
    outs_v[0][...] = ig[0:5, :]
    stores[0].start()
    keep = keep_hidden[...].astype(F32)
    for n in range(2):
        kept = jnp.broadcast_to(keep[n : n + 1, :], (16, 448))
        grad = grad_hidden[n]
        outs_v[1][n] = 0.9 * kept * first_hidden[n] + 0.1 * grad
        outs_v[2][n] = 0.999 * kept * second_hidden[n] + 0.001 * grad * grad
    stores[1].start()
    stores[2].start()
    kept = jnp.broadcast_to(keep_down[...].astype(F32), (2, 1024))
    grad = grad_down[...]
    outs_v[3][...] = 0.9 * kept * first_down[...] + 0.1 * grad
    outs_v[4][...] = 0.999 * kept * second_down[...] + 0.001 * grad * grad
    stores[3].start()
    stores[4].start()
    for copy in stores:
        copy.wait()


def body(
    tokens, cotangent, gate_weight, up_weight, down_weight, old_in_hidden, old_out_hidden, old_in_down,
    old_out_down, new_in_hidden, new_in_down, first_hidden, second_hidden, first_down, second_down,
    keep_hidden, keep_down,
):
    vmem = pl.BlockSpec(memory_space=pltpu.VMEM)
    far = pl.BlockSpec(memory_space=pltpu.HBM)
    ig, grad_hidden, grad_down = pl.pallas_call(
        kernel,
        out_shape=(
            jax.ShapeDtypeStruct((8, 1024), BF16),
            jax.ShapeDtypeStruct((2, 16, 448), F32),
            jax.ShapeDtypeStruct((2, 1024), F32),
        ),
        in_specs=[far] * len(INPUTS),
        out_specs=(vmem, vmem, vmem),
        scratch_shapes=[pltpu.VMEM(shape, BF16) for shape in INPUTS.values()]
        + [pltpu.VMEM(*spec) for spec in SCRATCH.values()]
        + [pltpu.SemaphoreType.DMA((N_SEM,)), pltpu.SemaphoreType.DMA((N_SEM,)), pltpu.SemaphoreType.DMA((len(INPUTS),))],
        compiler_params=pltpu.CompilerParams(
            collective_id=0, has_side_effects=True, vmem_limit_bytes=63 * 2**20
        ),
        cost_estimate=pl.CostEstimate(flops=2_000_000_000, bytes_accessed=4_000_000, transcendentals=150_000),
        name="layer",
    )(
        tokens, cotangent, gate_weight.T, up_weight.T, down_weight, old_in_hidden, old_out_hidden.transpose(0, 2, 1),
        old_in_down, old_out_down, new_in_hidden, new_in_down,
    )
    sources = (
        ig, grad_hidden, grad_down, first_hidden, second_hidden, first_down, second_down, keep_hidden,
        keep_down.reshape(1, 1024),
    )
    results = (
        jax.ShapeDtypeStruct((5, 1024), BF16),
        jax.ShapeDtypeStruct((2, 16, 448), F32),
        jax.ShapeDtypeStruct((2, 16, 448), F32),
        jax.ShapeDtypeStruct((2, 1024), F32),
        jax.ShapeDtypeStruct((2, 1024), F32),
    )
    return pl.pallas_call(
        moments,
        out_shape=results,
        in_specs=[far] * len(sources),
        out_specs=[far] * len(results),
        scratch_shapes=[pltpu.VMEM(a.shape, a.dtype) for a in sources + results]
        + [pltpu.SemaphoreType.DMA((len(sources),)), pltpu.SemaphoreType.DMA((len(results),))],
        compiler_params=pltpu.CompilerParams(vmem_limit_bytes=63 * 2**20),
        name="moments",
    )(*sources)


def solution(mesh):
    return jax.shard_map(
        body,
        mesh=mesh,
        in_specs=(
            P("row", "col"), P("row", "col"), P("col", "row"), P("col", "row"), P("row", "col"),
            P(None, "col", None), P(None, None, "row"), P("row", None), P(None, "col"), P(None, "col", None),
            P("row", None), P(None, "col", "row"), P(None, "col", "row"), P("row", "col"), P("row", "col"),
            P(None, "row"), P("col"),
        ),
        out_specs=(
            P("row", "col"), P(None, "col", "row"), P(None, "col", "row"), P("row", "col"), P("row", "col"),
        ),
        check_vma=False,
    )
```
